128 devices in a mesh: xs: 16 (over y, z), ys: 8 (over x, core).
Axes of the slice: x: 4, y: 4, z: 4, core: 2. Of those that a mesh axis runs over, the one named last changes fastest.
Arguments:
- multipoles: bfloat16 [121, 16384], P(None, ('xs', 'ys')), may hold values from -6 to 6
- translation_ops: bfloat16 [316, 121, 121], replicated, may hold values from -0.046875 to 0.046875
- target_interaction_table: int32 [316, 16384], P(None, ('xs', 'ys')), may hold values from -1 to 1151, as said below
- evaluation: bfloat16 [4, 121, 262144], P(None, None, ('xs', 'ys')), may hold values from -0.5 to 0.5
- ion_data: bfloat16 [4, 262144], P(None, ('xs', 'ys')), may hold values from -1 to 1
- atom_owner: int32 [262144, 1], P(('xs', 'ys')), may hold values from 0 to 127, as said below
- atom_slot: int32 [262144], P(('xs', 'ys')), may hold values from 0 to 127
Outputs:
- local_exp: bfloat16 [121, 16384], P(None, ('xs', 'ys'))
- atom_far_field: float32 [4, 262144], P(None, ('xs', 'ys'))
- box_virial: float32 [9, 16384], P(None, ('xs', 'ys'))
The draws below stay inside these ranges and needn't reach their ends.
Inputs may be any that keep to these rules, and one draw needn't show every extreme that they name: `target_interaction_table`: box slot s of a device is (bx * 4 + by) * 8 + bz; device (ix, iy) holds the periodic grid's boxes of x from ix * 4, y from iy * 4 and all z. Row k stands for the k-th offset (dx, dy, dz) of -3..3 in each coordinate, dx slowest, dz fastest, leaving out those with all three of magnitude 1 or less. An entry is -1, or (3 * (ex + 1) + (ey + 1)) * 128 + s naming the box at that offset from the target: slot s of the device ex steps along xs and ey steps along ys away, ex and ey in -1, 0, 1. It is -1 where the offset along some coordinate lies outside -2 - q .. 3 - q, q the parity of the target's coordinate there, and where the box at that offset holds no ions; most boxes hold ions. `atom_owner`: the device is ix * 8 + iy; an atom held by device (ix, iy) names that device itself or one of the eight devices ((ix + ex) mod 16, (iy + ey) mod 8) with ex, ey in -1, 0, 1; among the atoms of one device at most 32 name the same other device, and in every device's atoms some other device is named exactly 32 times.
All inputs are finite; a program needn't handle non-finite values.
Results may differ from the reference program's by a relative error of at most 0.0029.
Values may be sent and summed in bfloat16 or wider, within the bound.
A program may use at most 64 MiB of HBM per device.

```python
import jax
import jax.numpy as jnp
import numpy as np
from jax import lax

P_SIZE = 121
NOFF = 316
BXD = 4
BYD = 4
BZ = 8
ATOMS_DEV = 2048
CAP = 128
NBOX = 16384
ATOMS = 262144
SEND = 32
GX = 64
GY = 32
N_XS = 16
N_YS = 8
DEVICES = 128


def offset_table():
    listed = []
    for shift_x in range(-3, 4):
        for shift_y in range(-3, 4):
            for shift_z in range(-3, 4):
                if max(abs(shift_x), abs(shift_y), abs(shift_z)) >= 2:
                    listed.append((shift_x, shift_y, shift_z))
    return np.array(listed, dtype=np.int32)


def inside_list(coord, delta):
    parity = coord % 2
    return (delta >= -2 - parity) & (delta <= 3 - parity)


def draw_target_interaction_table(key, part):
    table = jnp.asarray(offset_table())
    filled = jax.random.randint(jax.random.fold_in(key, 7), (GX, GY, BZ), 0, 10) < 7
    targets = jnp.arange(NBOX, dtype=jnp.int32)
    device = targets // CAP
    home_x = (device // N_YS)[None, :]
    home_y = (device % N_YS)[None, :]
    slot = targets % CAP
    box_x = (slot // (BYD * BZ))[None, :]
    box_y = (slot // BZ % BYD)[None, :]
    box_z = (slot % BZ)[None, :]
    delta_x = table[:, 0:1]
    delta_y = table[:, 1:2]
    delta_z = table[:, 2:3]
    valid = inside_list(box_x, delta_x) & inside_list(box_y, delta_y) & inside_list(box_z, delta_z)
    reach_x = box_x + delta_x
    reach_y = box_y + delta_y
    step_x = jnp.floor_divide(reach_x, BXD)
    stride_along_y = jnp.floor_divide(reach_y, BYD)
    source_x = reach_x - step_x * BXD
    source_y = reach_y - stride_along_y * BYD
    source_z = jnp.remainder(box_z + delta_z, BZ)
    global_x = jnp.remainder(home_x * BXD + reach_x, GX)
    global_y = jnp.remainder(home_y * BYD + reach_y, GY)
    held = filled[global_x, global_y, source_z]
    entry = (3 * (step_x + 1) + (stride_along_y + 1)) * CAP + (source_x * BYD + source_y) * BZ + source_z
    return jnp.where(valid & held, entry, -1).astype(jnp.int32)


def neighbour_shifts():
    listed = []
    for shift_x in (-1, 0, 1):
        for shift_y in (-1, 0, 1):
            if shift_x != 0 or shift_y != 0:
                listed.append((shift_x, shift_y))
    return np.array(listed, dtype=np.int32)


def draw_atom_owner(key, part):
    shifts = jnp.asarray(neighbour_shifts())

    def one_device(device):
        own_key = jax.random.fold_in(key, device)
        counts = jax.random.randint(jax.random.fold_in(own_key, 1), (8,), SEND // 2, SEND + 1)
        fullest = jax.random.randint(jax.random.fold_in(own_key, 2), (), 0, 8)
        counts = jnp.where(jnp.arange(8, dtype=jnp.int32) == fullest, SEND, counts).astype(jnp.int32)
        ends = jnp.cumsum(counts)
        position = jnp.arange(ATOMS_DEV, dtype=jnp.int32)
        which = jnp.sum((position[:, None] >= ends[None, :]).astype(jnp.int32), axis=1)
        home_x = device // N_YS
        home_y = device % N_YS
        nearby = (home_x + shifts[:, 0]) % N_XS * N_YS + (home_y + shifts[:, 1]) % N_YS
        choices_all = jnp.concatenate([nearby, jnp.reshape(device, (1,))]).astype(jnp.int32)
        owners = choices_all[which]
        order = jax.random.permutation(jax.random.fold_in(own_key, 3), ATOMS_DEV)
        return owners[order]
    owners = jax.vmap(one_device)(jnp.arange(DEVICES, dtype=jnp.int32))
    return owners.reshape(ATOMS, 1).astype(jnp.int32)


def place_ends(result, key, smallest, high):
    longest = result.shape.index(max(result.shape))
    spots = []
    for shift in (0, 1):
        where = [jax.random.randint(jax.random.fold_in(key, axis), (), 0, length) for axis, length in enumerate(result.shape)]
        where[longest] = (where[longest] + shift) % result.shape[longest]
        spots.append(tuple(where))
    return result.at[spots[0]].set(smallest).at[spots[1]].set(high)


def shard_levels(key, extent, pieces, least, high):
    def one(axis_at, blocks):
        steps = jax.random.uniform(jax.random.fold_in(jax.random.fold_in(key, 6), axis_at), (blocks,), jnp.float32, least / len(pieces), high / len(pieces))
        return jnp.repeat(jnp.exp(steps), extent[axis_at] // blocks).reshape((-1,) + (1,) * (len(extent) - axis_at - 1))

    loudness = one(*pieces[0])
    for cut in pieces[1:]:
        loudness = loudness * one(*cut)
    return loudness


def scatter_about(key, shape, spread, most, shards=(), kind=jnp.bfloat16):
    values = spread * jax.random.normal(key, shape, jnp.float32)
    if shards:
        values = values * shard_levels(key, shape, shards, -0.22, 0.18)
    return jnp.clip(values, -most, most).astype(kind)


def setup_inputs(seed: int = 0) -> dict:
    streams_of = jax.random.split(jax.random.key(seed), 8)
    return {
        "multipoles": scatter_about(streams_of[0], (P_SIZE, NBOX), 1.0, 6.0, ((1, 128),)),
        "translation_ops": scatter_about(streams_of[1], (NOFF, P_SIZE, P_SIZE), (P_SIZE * 132) ** -0.5, 0.046875),
        "target_interaction_table": draw_target_interaction_table(jax.random.fold_in(streams_of[7], 71), 0),
        "evaluation": scatter_about(streams_of[3], (4, P_SIZE, ATOMS), P_SIZE ** -0.5, 0.5, ((2, 128),)),
        "ion_data": jnp.clip(jax.random.uniform(streams_of[4], (4, ATOMS), jnp.float32, -1.0, 1.0) * shard_levels(streams_of[4], (4, ATOMS), ((1, 128),), -0.4, 0.0), -1.0, 1.0).astype(jnp.bfloat16),
        "atom_owner": draw_atom_owner(jax.random.fold_in(streams_of[7], 71), 0),
        "atom_slot": place_ends(jax.random.randint(streams_of[6], (ATOMS,), 0, CAP), jax.random.fold_in(streams_of[6], 1), 0, CAP - 1).astype(jnp.int32),
    }


def reference(multipoles, translation_ops, target_interaction_table, evaluation, ion_data, atom_owner, atom_slot):
    nbox = multipoles.shape[1]
    targets = jnp.arange(nbox, dtype=jnp.int32)
    device = targets // CAP
    home_x = device // N_YS
    home_y = device % N_YS
    padded = jnp.concatenate([multipoles.astype(jnp.float32), jnp.zeros((P_SIZE, 1), jnp.float32)], axis=1)

    def step(total, item):
        translation_matrix, entries = item
        valid = entries >= 0
        safe = jnp.where(valid, entries, 0).astype(jnp.int32)
        shift_x = safe // (3 * CAP) - 1
        shift_y = (safe // CAP) % 3 - 1
        source_dev = ((home_x + shift_x) % N_XS) * N_YS + (home_y + shift_y) % N_YS
        source_box_index = jnp.where(valid, source_dev * CAP + safe % CAP, nbox).astype(jnp.int32)
        gathered = jnp.take(padded, source_box_index, axis=1)
        return total + jnp.dot(translation_matrix.astype(jnp.float32), gathered), None

    total, _ = lax.scan(step, jnp.zeros((P_SIZE, nbox), jnp.float32), (translation_ops, target_interaction_table))
    local_exp = total.astype(jnp.bfloat16)

    box = (atom_owner[:, 0] * CAP + atom_slot).astype(jnp.int32)
    box_cols = jnp.take(local_exp, box, axis=1).astype(jnp.float32)
    atom_far_field = jnp.stack([jnp.sum(evaluation[c].astype(jnp.float32) * box_cols, axis=0) for c in range(4)])

    charge = ion_data[0].astype(jnp.float32)
    position = ion_data[1:4].astype(jnp.float32)
    virial_terms = (charge[None, None, :] * position[:, None, :] * atom_far_field[None, 1:4, :]).reshape(9, -1)
    box_virial = jax.ops.segment_sum(virial_terms.T, box, num_segments=nbox).T
    return local_exp, atom_far_field, box_virial
```

```python
import functools

import jax
import jax.numpy as jnp
from jax import lax
from jax.experimental import pallas as pl
from jax.experimental.pallas import tpu as pltpu
from jax.sharding import PartitionSpec as P

MESH = pl.DeviceIdType.MESH
NT = (((1,), (1,)), ((), ()))
NN = (((1,), (0,)), ((), ()))
F32 = jnp.float32
BF16 = jnp.bfloat16

AROUND = [(ex, ey) for ex in (-1, 0, 1) for ey in (-1, 0, 1) if (ex, ey) != (0, 0)]


def offset_columns():
    listed, row = [], 0
    for dx in range(-3, 4):
        for dy in range(-3, 4):
            near = abs(dx) <= 1 and abs(dy) <= 1
            listed.append((dx, dy, row, near))
            row += 4 if near else 7
    return listed


COLUMNS = offset_columns()
SELF_ROW = [c[2] for c in COLUMNS if c[:2] == (0, 0)][0] + 1
CHUNKS = [(0, 32), (32, 32), (64, 32), (96, 25)]


def iota(shape, axis):
    return lax.broadcasted_iota(jnp.int32, shape, axis)


def one_hot(condition):
    return jnp.where(condition, 1.0, 0.0).astype(BF16)


def mirror_z(x):
    axis = x.ndim - 1
    lane = iota(x.shape, axis)
    for bit in (1, 2, 4):
        x = jnp.where((lane & bit) != 0, pltpu.roll(x, bit, axis), pltpu.roll(x, 128 - bit, axis))
    return x


def kernel(
    nx, ny,
    mult, ops, table, ev, ions, owner, slot,
    local_out, field_out, virial_out,
    mraw, trow, iraw, oraw, sraw, eb, tb, F, Ef, R, OH, ext, G,
    msend, mrecv, ec, gmsg, fg, ret, Lrep, fo,
    in_sem, op_sem, s1, r1, s2, r2, s3, r3,
):
    mx = lax.axis_index("xs")
    my = lax.axis_index("ys")

    def peer(g):
        ex, ey = AROUND[g]
        return (lax.rem(mx + ex + nx, nx), lax.rem(my + ey + ny, ny))

    first = SELF_ROW // 8 * 8
    loads = [
        pltpu.make_async_copy(mult, mraw, in_sem.at[0]),
        pltpu.make_async_copy(table.at[pl.ds(first, 8)], trow, in_sem.at[1]),
        pltpu.make_async_copy(owner, oraw, in_sem.at[2]),
        pltpu.make_async_copy(slot, sraw, in_sem.at[3]),
        pltpu.make_async_copy(ions, iraw, in_sem.at[4]),
        pltpu.make_async_copy(ev, eb, in_sem.at[5]),
    ]
    for copy in loads:
        copy.start()
    op_loads = [
        pltpu.make_async_copy(ops.at[pl.ds(q0, n)], tb.at[pl.ds(q0, n)], op_sem.at[c])
        for c, (q0, n) in enumerate(CHUNKS)
    ]
    for copy in op_loads:
        copy.start()

    barrier = pltpu.get_barrier_semaphore()
    for g in range(8):
        pl.semaphore_signal(barrier, inc=1, device_id=peer(g), device_id_type=MESH)

    loads[0].wait()
    loads[1].wait()
    named = trow[SELF_ROW - first:SELF_ROW - first + 1, :]
    lane = iota((1, 128), 1)
    named = jnp.where((lane & 7) < 6, pltpu.roll(named, 126, 1), pltpu.roll(named, 6, 1))
    filled = named >= 0
    pick = one_hot((iota((128, 128), 0) == (iota((128, 128), 1) ^ 7)) & jnp.broadcast_to(filled, (128, 128)))
    turned = lax.dot_general(pick, mraw[...], NT, preferred_element_type=F32)
    msend[...] = jnp.zeros_like(msend)
    msend[:, 0:121] = turned.astype(BF16)

    pl.semaphore_wait(barrier, 8)
    halo = []
    for g in range(8):
        ex = AROUND[g][0]
        rows = pl.ds(32 if ex < 0 else 0, 128 if ex == 0 else 96)
        halo.append(pltpu.make_async_remote_copy(
            src_ref=msend.at[rows], dst_ref=mrecv.at[g, rows], send_sem=s1.at[g], recv_sem=r1.at[g],
            device_id=peer(7 - g), device_id_type=MESH))
        halo[-1].start()

    loads[2].wait()
    loads[3].wait()
    own_id = oraw[...]
    shift = ny.bit_length() - 1
    step_x = (((own_id >> shift) - mx + 1 + nx) & (nx - 1)) - 1
    step_y = (((own_id & (ny - 1)) - my + 1 + ny) & (ny - 1)) - 1
    towards = 3 * (step_x + 1) + step_y + 1
    here = towards == 4
    group = jnp.where(here, -1, 7 - jnp.where(towards > 4, towards - 1, towards))
    member = jnp.where(iota((8, 2048), 0) == group, 1.0, 0.0)
    stacked = jnp.concatenate([member[:, 128 * b:128 * b + 128] for b in range(16)], axis=0)
    stacked_b = stacked.astype(BF16)
    row, col = iota((128, 128), 0), iota((128, 128), 1)
    before = one_hot(row < col)
    earlier = one_hot(((row & 7) == (col & 7)) & ((col >> 3) < (row >> 3)))
    ones = jnp.ones((128, 128), BF16)
    counts = lax.dot_general(earlier, stacked_b, NN, preferred_element_type=F32).astype(BF16)
    rank = lax.dot_general(stacked_b, before, NN, preferred_element_type=F32)
    rank = rank + lax.dot_general(counts, ones, NN, preferred_element_type=F32)
    place = stacked * (rank + (32 * (row & 7) + 1).astype(F32))
    place = jnp.sum(place.reshape(16, 8, 128), axis=1, keepdims=True) - 1.0
    row_f = iota((256, 128), 0).astype(F32)
    for b in range(16):
        R[:, 128 * b:128 * b + 128] = one_hot(row_f == place[b])
    own_slot = sraw[...]
    OH[:, 0:2048] = one_hot(iota((128, 2048), 0) == jnp.where(here, own_slot ^ 7, -1))

    loads[4].wait()
    loads[5].wait()

    def spread(i, _):
        both = jnp.concatenate([eb[2 * i].astype(F32), eb[2 * i + 1].astype(F32)], axis=0)
        Ef[pl.ds(pl.multiple_of(8 * i, 8), 8), 0:2048] = both
        return 0

    lax.fori_loop(0, 60, spread, 0, unroll=4)
    Ef[480:488, 0:2048] = jnp.concatenate([eb[120].astype(F32), iraw[...].astype(F32)], axis=0)
    Ef[488:496, 0:2048] = jnp.where(iota((8, 2048), 0) == 0, own_slot.astype(F32), 0.0)
    Ef[496:512, 0:2048] = jnp.zeros((16, 2048), F32)

    ec[...] = lax.dot_general(
        R[...], Ef[:, 0:2048].astype(BF16), NT, preferred_element_type=F32).astype(BF16)
    guests = []
    for g in range(8):
        rows = pl.ds(32 * g, 32)
        guests.append(pltpu.make_async_remote_copy(
            src_ref=ec.at[rows], dst_ref=gmsg.at[rows], send_sem=s2.at[g], recv_sem=r2.at[g],
            device_id=peer(7 - g), device_id_type=MESH))
        guests[-1].start()

    def widen(c):
        q0, n = CHUNKS[c]
        op_loads[c].wait()
        F[q0:q0 + n, 0:316, 0:121] = tb[q0:q0 + n].astype(F32)

    widen(0)

    def place_block(block, ex, ey):
        block = block.astype(F32).reshape(4, 4, 8, 128)
        sx = {-1: (1, 4, 0), 0: (0, 4, 3), 1: (0, 3, 7)}[ex]
        sy = {-1: (1, 4, 0), 0: (0, 4, 3), 1: (0, 3, 7)}[ey]
        ext[sx[2]:sx[2] + sx[1] - sx[0], sy[2]:sy[2] + sy[1] - sy[0]] = block[sx[0]:sx[1], sy[0]:sy[1]]

    place_block(msend[...], 0, 0)
    for g in range(8):
        halo[g].wait_recv()
        place_block(mrecv[g], *AROUND[g])
    grid_x, grid_y = iota((4, 4, 8, 128), 0), iota((4, 4, 8, 128), 1)
    for j, (dx, dy, _, _) in enumerate(COLUMNS):
        block = ext[dx + 3:dx + 7, dy + 3:dy + 7]
        if abs(dx) == 3:
            block = jnp.where((grid_x & 1) == (0 if dx > 0 else 1), block, 0.0)
        if abs(dy) == 3:
            block = jnp.where((grid_y & 1) == (0 if dy > 0 else 1), block, 0.0)
        G[:, 128 * j:128 * j + 128] = block.reshape(128, 128).astype(BF16)

    cell = (32, 8, 128)
    dz = iota(cell, 1) - 3
    source_z = (iota(cell, 2) & 7) - dz
    inside = (source_z >= 0) & (source_z <= 7)
    odd_z = (iota(cell, 2) & 1) == 0
    valid = (jnp.abs(dz) < 3) | ((dz == -3) & odd_z) | ((dz == 3) & jnp.logical_not(odd_z))
    slots = iota((32, 8, 128), 1)
    in_terms = iota((32, 8, 128), 2) < 121

    def weights(q0, j):
        _, _, k0, near = COLUMNS[j]
        rows = F[q0:q0 + 32, k0:k0 + 8, :]
        if near:
            upper = F[q0:q0 + 32, k0 - 3:k0 + 5, :]
            rows = jnp.where(slots < 2, rows, jnp.where((slots >= 5) & (slots < 7), upper, 0.0))
        return jnp.where(in_terms, rows, 0.0).reshape(256, 128).astype(BF16)

    def translate(c):
        q0, n = CHUNKS[c]
        total = jnp.zeros((256, 128), F32)
        for j in range(0, 49, 2):
            if j + 1 < 49:
                w = jnp.concatenate([weights(q0, j), weights(q0, j + 1)], axis=1)
                total = total + lax.dot_general(w, G[:, 128 * j:128 * j + 256], NT, preferred_element_type=F32)
            else:
                total = total + lax.dot_general(
                    weights(q0, j), G[:, 128 * j:128 * j + 128], NT, preferred_element_type=F32)
        total = total.reshape(cell)
        skewed = pltpu.roll(total, 0, 2, stride=1, stride_axis=1)
        turned = pltpu.roll(skewed, 125, 2)
        wrapped = jnp.where(dz > 0, pltpu.roll(skewed, 117, 2), pltpu.roll(skewed, 5, 2))
        picked = jnp.where(valid, jnp.where(inside, turned, wrapped), 0.0)
        sums = jnp.sum(picked, axis=1, keepdims=True)
        wide = jnp.broadcast_to(sums, cell).reshape(16, 2, 8, 128)
        wide = jnp.where(iota((16, 8, 128), 1) < 4, wide[:, 0], wide[:, 1]).reshape(128, 128)
        if n < 32:
            wide = jnp.where(iota((128, 128), 0) < 4 * n, wide, 0.0)
        Lrep[4 * q0:4 * q0 + 128, :] = wide.astype(BF16)
        return jnp.sum(picked, axis=1)

    def put_local(c, sums):
        q0, n = CHUNKS[c]
        local_out[q0:q0 + n, :] = mirror_z(sums)[0:n].astype(BF16)

    F[121:128] = jnp.zeros((7, 320, 128), F32)
    for c in range(3):
        if c:
            widen(c)
        put_local(c, translate(c))
    widen(3)

    for g in range(8):
        guests[g].wait_recv()
    received = gmsg[...].astype(F32)
    for c in range(4):
        Ef[128 * c:128 * c + 128, 2048:2304] = jnp.transpose(received[:, 128 * c:128 * c + 128])
    guest_slot = Ef[488:489, 2048:2304].astype(jnp.int32) ^ 7
    OH[:, 2048:2304] = one_hot(iota((128, 256), 0) == guest_slot)

    last = translate(3)

    def evaluate(start):
        values = lax.dot_general(
            Lrep[0:496, :], OH[:, start:start + 256], NN, preferred_element_type=F32)
        values = values * Ef[0:496, start:start + 256]
        total = jnp.sum(values.reshape(62, 8, 256), axis=0)
        return total + pltpu.roll(total, 4, 0)

    far = evaluate(2048)
    fo[:, 2048:2304] = far
    fg[0] = far[:, 0:128]
    fg[1] = far[:, 128:256]
    answers = []
    for g in range(8):
        answers.append(pltpu.make_async_remote_copy(
            src_ref=fg.at[g // 4], dst_ref=ret.at[g], send_sem=s3.at[g], recv_sem=r3.at[g],
            device_id=peer(g), device_id_type=MESH))
        answers[-1].start()
    put_local(3, last)
    for b in range(8):
        fo[:, 256 * b:256 * b + 256] = evaluate(256 * b)

    field = fo[...]
    charge = Ef[484:485, :]
    low = iota((8, 2304), 0) < 4
    arm = jnp.where(low, charge * Ef[485:486, :], charge * Ef[486:487, :])
    terms = jnp.concatenate([arm * field, charge * Ef[487:488, :] * field], axis=0)
    high = terms.astype(BF16)
    rest = (terms - high.astype(F32)).astype(BF16)
    sums = lax.dot_general(jnp.concatenate([high, rest], axis=0), OH[...], NT, preferred_element_type=F32)
    sums = mirror_z(sums[0:16] + sums[16:32])
    for a in range(3):
        virial_out[3 * a:3 * a + 3, :] = sums[4 * a + 1:4 * a + 4]

    for g in range(8):
        answers[g].wait_recv()
    quarter = iota((8, 128), 1) >> 5
    tiles = []
    for u in range(2):
        tile = ret[4 * u]
        for v in range(1, 4):
            tile = jnp.where(quarter == v, ret[4 * u + v], tile)
        tiles.append(tile)
    back = jnp.concatenate(tiles, axis=1)
    parts = []
    for _ in range(3):
        parts.append(back.astype(BF16).astype(F32))
        back = back - parts[-1]
    spread_out = lax.dot_general(
        jnp.concatenate(parts, axis=0).astype(BF16), R[...], NN, preferred_element_type=F32)
    total = fo[:, 0:2048] + spread_out[0:8] + spread_out[8:16] + spread_out[16:24]
    field_out[...] = total[0:4]

    for g in range(8):
        halo[g].wait_send()
        guests[g].wait_send()
        answers[g].wait_send()


def shards(mult, ops, table, ev, ions, owner, slot):
    nx, ny = lax.axis_size("xs"), lax.axis_size("ys")
    dma = pltpu.SemaphoreType.DMA
    vmem = pltpu.VMEM
    return pl.pallas_call(
        functools.partial(kernel, nx, ny),
        out_shape=(
            jax.ShapeDtypeStruct((121, 128), BF16),
            jax.ShapeDtypeStruct((4, 2048), F32),
            jax.ShapeDtypeStruct((9, 128), F32),
        ),
        in_specs=[pl.BlockSpec(memory_space=pl.ANY)] * 7,
        out_specs=[pl.BlockSpec(memory_space=pltpu.VMEM)] * 3,
        scratch_shapes=[
            vmem((121, 128), BF16), vmem((8, 128), jnp.int32), vmem((4, 2048), BF16),
            vmem((1, 2048), jnp.int32), vmem((1, 2048), jnp.int32),
            vmem((121, 4, 2048), BF16), vmem((121, 316, 121), BF16), vmem((128, 320, 128), F32),
            vmem((512, 2304), F32), vmem((256, 2048), BF16), vmem((128, 2304), BF16),
            vmem((10, 10, 8, 128), F32), vmem((128, 49 * 128), BF16),
            vmem((128, 128), BF16), vmem((8, 128, 128), BF16), vmem((256, 512), BF16), vmem((256, 512), BF16),
            vmem((2, 8, 128), F32), vmem((8, 8, 128), F32), vmem((512, 128), BF16), vmem((8, 2304), F32),
            dma((6,)), dma((4,)), dma((8,)), dma((8,)), dma((8,)), dma((8,)), dma((8,)), dma((8,)),
        ],
        compiler_params=pltpu.CompilerParams(
            collective_id=0, has_side_effects=True, vmem_limit_bytes=58 * 2**20),
    )(
        mult,
        jnp.transpose(ops, (1, 0, 2)),
        table,
        jnp.transpose(ev, (1, 0, 2)),
        ions,
        jnp.reshape(owner, (1, owner.shape[0])),
        jnp.reshape(slot, (1, slot.shape[0])),
    )


def solution(mesh):
    both = ("xs", "ys")
    placed = (
        P(None, both),
        P(),
        P(None, both),
        P(None, None, both),
        P(None, both),
        P(both, None),
        P(both),
    )
    return jax.shard_map(
        shards,
        mesh=mesh,
        in_specs=placed,
        out_specs=(P(None, both), P(None, both), P(None, both)),
        check_vma=False,
    )
```

```python
import functools

import jax
import jax.numpy as jnp
from jax import lax
from jax.experimental import pallas as pl
from jax.experimental.pallas import tpu as pltpu
from jax.sharding import PartitionSpec as P

MESH = pl.DeviceIdType.MESH
NT = (((1,), (1,)), ((), ()))
NN = (((1,), (0,)), ((), ()))
F32 = jnp.float32
BF16 = jnp.bfloat16

AROUND = [(ex, ey) for ex in (-1, 0, 1) for ey in (-1, 0, 1) if (ex, ey) != (0, 0)]


def offset_columns():
    listed, row = [], 0
    for dx in range(-3, 4):
        for dy in range(-3, 4):
            near = abs(dx) <= 1 and abs(dy) <= 1
            listed.append((dx, dy, row, near))
            row += 4 if near else 7
    return listed


COLUMNS = offset_columns()
SELF_ROW = [c[2] for c in COLUMNS if c[:2] == (0, 0)][0] + 1
CHUNKS = [(0, 32), (32, 32), (64, 32), (96, 25)]
STEPS = 25


def iota(shape, axis):
    return lax.broadcasted_iota(jnp.int32, shape, axis)


def one_hot(condition):
    return jnp.where(condition, 1.0, 0.0).astype(BF16)


def mirror_z(x):
    axis = x.ndim - 1
    lane = iota(x.shape, axis)
    for bit in (1, 2, 4):
        x = jnp.where((lane & bit) != 0, pltpu.roll(x, bit, axis), pltpu.roll(x, 128 - bit, axis))
    return x


def kernel(
    nx, ny,
    mult, ops, table, ev, ions, owner, slot,
    local_out, field_out, virial_out,
    mraw, trow, iraw, oraw, sraw, eb, tb, F, Ef, R, OH, ext, G,
    msend, mrecv, ec, gmsg, fg, ret, Lrep, fo,
    in_sem, op_sem, s1, r1, s2, r2, s3, r3,
):
    mx = lax.axis_index("xs")
    my = lax.axis_index("ys")

    def peer(g):
        ex, ey = AROUND[g]
        return (lax.rem(mx + ex + nx, nx), lax.rem(my + ey + ny, ny))

    first = SELF_ROW // 8 * 8
    loads = [
        pltpu.make_async_copy(mult, mraw, in_sem.at[0]),
        pltpu.make_async_copy(table.at[pl.ds(first, 8)], trow, in_sem.at[1]),
        pltpu.make_async_copy(owner, oraw, in_sem.at[2]),
        pltpu.make_async_copy(slot, sraw, in_sem.at[3]),
        pltpu.make_async_copy(ions, iraw, in_sem.at[4]),
        pltpu.make_async_copy(ev, eb, in_sem.at[5]),
    ]
    for copy in loads:
        copy.start()
    op_loads = [
        pltpu.make_async_copy(ops.at[pl.ds(q0, n)], tb.at[pl.ds(q0, n)], op_sem.at[c])
        for c, (q0, n) in enumerate(CHUNKS)
    ]
    for copy in op_loads:
        copy.start()

    barrier = pltpu.get_barrier_semaphore()
    for g in range(8):
        pl.semaphore_signal(barrier, inc=1, device_id=peer(g), device_id_type=MESH)

    loads[0].wait()
    loads[1].wait()
    named = trow[SELF_ROW - first:SELF_ROW - first + 1, :]
    lane = iota((1, 128), 1)
    named = jnp.where((lane & 7) < 6, pltpu.roll(named, 126, 1), pltpu.roll(named, 6, 1))
    filled = named >= 0
    pick = one_hot((iota((128, 128), 0) == (iota((128, 128), 1) ^ 7)) & jnp.broadcast_to(filled, (128, 128)))
    turned = lax.dot_general(pick, mraw[...], NT, preferred_element_type=F32)
    msend[...] = jnp.zeros_like(msend)
    msend[:, 0:121] = turned.astype(BF16)

    pl.semaphore_wait(barrier, 8)
    halo = []
    for g in range(8):
        ex = AROUND[g][0]
        rows = pl.ds(32 if ex < 0 else 0, 128 if ex == 0 else 96)
        halo.append(pltpu.make_async_remote_copy(
            src_ref=msend.at[rows], dst_ref=mrecv.at[g, rows], send_sem=s1.at[g], recv_sem=r1.at[g],
            device_id=peer(7 - g), device_id_type=MESH))
        halo[-1].start()

    loads[2].wait()
    loads[3].wait()
    own_id = oraw[...]
    shift = ny.bit_length() - 1
    step_x = (((own_id >> shift) - mx + 1 + nx) & (nx - 1)) - 1
    step_y = (((own_id & (ny - 1)) - my + 1 + ny) & (ny - 1)) - 1
    towards = 3 * (step_x + 1) + step_y + 1
    here = towards == 4
    group = jnp.where(here, -1, 7 - jnp.where(towards > 4, towards - 1, towards))
    member = jnp.where(iota((8, 2048), 0) == group, 1.0, 0.0)
    stacked = jnp.concatenate([member[:, 128 * b:128 * b + 128] for b in range(16)], axis=0)
    stacked_b = stacked.astype(BF16)
    row, col = iota((128, 128), 0), iota((128, 128), 1)
    before = one_hot(row < col)
    earlier = one_hot(((row & 7) == (col & 7)) & ((col >> 3) < (row >> 3)))
    ones = jnp.ones((128, 128), BF16)
    counts = lax.dot_general(earlier, stacked_b, NN, preferred_element_type=F32).astype(BF16)
    rank = lax.dot_general(stacked_b, before, NN, preferred_element_type=F32)
    rank = rank + lax.dot_general(counts, ones, NN, preferred_element_type=F32)
    place = stacked * (rank + (32 * (row & 7) + 1).astype(F32))
    place = jnp.sum(place.reshape(16, 8, 128), axis=1, keepdims=True) - 1.0
    row_f = iota((256, 128), 0).astype(F32)
    for b in range(16):
        R[:, 128 * b:128 * b + 128] = one_hot(row_f == place[b])
    own_slot = sraw[...]
    OH[:, 0:2048] = one_hot(iota((128, 2048), 0) == jnp.where(here, own_slot ^ 7, -1))

    loads[4].wait()
    loads[5].wait()

    def spread(i, _):
        both = jnp.concatenate([eb[2 * i].astype(F32), eb[2 * i + 1].astype(F32)], axis=0)
        Ef[pl.ds(pl.multiple_of(8 * i, 8), 8), 0:2048] = both
        return 0

    lax.fori_loop(0, 60, spread, 0, unroll=4)
    Ef[480:488, 0:2048] = jnp.concatenate([eb[120].astype(F32), iraw[...].astype(F32)], axis=0)
    Ef[488:496, 0:2048] = jnp.where(iota((8, 2048), 0) == 0, own_slot.astype(F32), 0.0)
    Ef[496:512, 0:2048] = jnp.zeros((16, 2048), F32)

    ec[...] = lax.dot_general(
        R[...], Ef[:, 0:2048].astype(BF16), NT, preferred_element_type=F32).astype(BF16)
    guests = []
    for g in range(8):
        rows = pl.ds(32 * g, 32)
        guests.append(pltpu.make_async_remote_copy(
            src_ref=ec.at[rows], dst_ref=gmsg.at[rows], send_sem=s2.at[g], recv_sem=r2.at[g],
            device_id=peer(7 - g), device_id_type=MESH))
        guests[-1].start()

    def widen(c, step):
        q0, n = CHUNKS[c]
        low, high = q0 + n * step // STEPS, q0 + n * (step + 1) // STEPS
        F[low:high, 0:316, 0:121] = tb[low:high].astype(F32)

    op_loads[0].wait()
    for step in range(STEPS):
        widen(0, step)

    def place_block(block, ex, ey):
        block = block.astype(F32).reshape(4, 4, 8, 128)
        sx = {-1: (1, 4, 0), 0: (0, 4, 3), 1: (0, 3, 7)}[ex]
        sy = {-1: (1, 4, 0), 0: (0, 4, 3), 1: (0, 3, 7)}[ey]
        ext[sx[2]:sx[2] + sx[1] - sx[0], sy[2]:sy[2] + sy[1] - sy[0]] = block[sx[0]:sx[1], sy[0]:sy[1]]

    place_block(msend[...], 0, 0)
    for g in range(8):
        halo[g].wait_recv()
        place_block(mrecv[g], *AROUND[g])
    grid_x, grid_y = iota((4, 4, 8, 128), 0), iota((4, 4, 8, 128), 1)
    for j, (dx, dy, _, _) in enumerate(COLUMNS):
        block = ext[dx + 3:dx + 7, dy + 3:dy + 7]
        if abs(dx) == 3:
            block = jnp.where((grid_x & 1) == (0 if dx > 0 else 1), block, 0.0)
        if abs(dy) == 3:
            block = jnp.where((grid_y & 1) == (0 if dy > 0 else 1), block, 0.0)
        G[:, 128 * j:128 * j + 128] = block.reshape(128, 128).astype(BF16)

    def weights(q0, n, j):
        _, _, k0, near = COLUMNS[j]
        shape = (n, 8, 128)
        rows = F[q0:q0 + n, k0:k0 + 8, :]
        if near:
            slots = iota(shape, 1)
            upper = F[q0:q0 + n, k0 - 3:k0 + 5, :]
            rows = jnp.where(slots < 2, rows, jnp.where((slots >= 5) & (slots < 7), upper, 0.0))
        return jnp.where(iota(shape, 2) < 121, rows, 0.0).reshape(8 * n, 128).astype(BF16)

    def translate(c, beside):
        q0, n = CHUNKS[c]
        n += n % 2
        total = jnp.zeros((8 * n, 128), F32)
        for step in range(STEPS):
            j = 2 * step
            w = weights(q0, n, j)
            width = 128
            if j + 1 < 49:
                w = jnp.concatenate([w, weights(q0, n, j + 1)], axis=1)
                width = 256
            total = total + lax.dot_general(w, G[:, 128 * j:128 * j + width], NT, preferred_element_type=F32)
            beside(step)
        return total

    def settle(c, total):
        q0, n = CHUNKS[c]
        rows = n + n % 2
        cell = (rows, 8, 128)
        dz = iota(cell, 1) - 3
        source_z = (iota(cell, 2) & 7) - dz
        inside = (source_z >= 0) & (source_z <= 7)
        odd_z = (iota(cell, 2) & 1) == 0
        valid = (jnp.abs(dz) < 3) | ((dz == -3) & odd_z) | ((dz == 3) & jnp.logical_not(odd_z))
        skewed = pltpu.roll(total.reshape(cell), 0, 2, stride=1, stride_axis=1)
        turned = pltpu.roll(skewed, 125, 2)
        wrapped = jnp.where(dz > 0, pltpu.roll(skewed, 117, 2), pltpu.roll(skewed, 5, 2))
        picked = jnp.where(valid, jnp.where(inside, turned, wrapped), 0.0)
        sums = jnp.sum(picked, axis=1, keepdims=True)
        wide = jnp.broadcast_to(sums, cell).reshape(rows // 2, 2, 8, 128)
        wide = jnp.where(iota((rows // 2, 8, 128), 1) < 4, wide[:, 0], wide[:, 1]).reshape(4 * rows, 128)
        if n < rows:
            wide = jnp.where(iota((4 * rows, 128), 0) < 4 * n, wide, 0.0)
            Lrep[4 * (q0 + rows):496, :] = jnp.zeros((496 - 4 * (q0 + rows), 128), BF16)
        Lrep[4 * q0:4 * (q0 + rows), :] = wide.astype(BF16)
        return jnp.sum(picked, axis=1)

    def put_local(c, sums):
        q0, n = CHUNKS[c]
        local_out[q0:q0 + n, :] = mirror_z(sums)[0:n].astype(BF16)

    F[121:122] = jnp.zeros((1, 320, 128), F32)
    done = None
    for c in range(3):
        op_loads[c + 1].wait()

        def beside(step):
            widen(c + 1, step)
            if step == 4 and done is not None:
                put_local(c - 1, settle(c - 1, done))

        done = translate(c, beside)

    for g in range(8):
        guests[g].wait_recv()
    received = gmsg[...].astype(F32)
    for c in range(4):
        Ef[128 * c:128 * c + 128, 2048:2304] = jnp.transpose(received[:, 128 * c:128 * c + 128])
    guest_slot = Ef[488:489, 2048:2304].astype(jnp.int32) ^ 7
    OH[:, 2048:2304] = one_hot(iota((128, 256), 0) == guest_slot)

    def beside_last(step):
        if step == 4:
            put_local(2, settle(2, done))

    last = settle(3, translate(3, beside_last))

    def evaluate(start):
        values = lax.dot_general(
            Lrep[0:496, :], OH[:, start:start + 256], NN, preferred_element_type=F32)
        values = values * Ef[0:496, start:start + 256]
        total = jnp.sum(values.reshape(62, 8, 256), axis=0)
        return total + pltpu.roll(total, 4, 0)

    far = evaluate(2048)
    fo[:, 2048:2304] = far
    fg[0] = far[:, 0:128]
    fg[1] = far[:, 128:256]
    answers = []
    for g in range(8):
        answers.append(pltpu.make_async_remote_copy(
            src_ref=fg.at[g // 4], dst_ref=ret.at[g], send_sem=s3.at[g], recv_sem=r3.at[g],
            device_id=peer(g), device_id_type=MESH))
        answers[-1].start()
    put_local(3, last)
    for b in range(8):
        fo[:, 256 * b:256 * b + 256] = evaluate(256 * b)

    field = fo[...]
    charge = Ef[484:485, :]
    low = iota((8, 2304), 0) < 4
    arm = jnp.where(low, charge * Ef[485:486, :], charge * Ef[486:487, :])
    terms = jnp.concatenate([arm * field, charge * Ef[487:488, :] * field], axis=0)
    high = terms.astype(BF16)
    rest = (terms - high.astype(F32)).astype(BF16)
    sums = lax.dot_general(jnp.concatenate([high, rest], axis=0), OH[...], NT, preferred_element_type=F32)
    sums = mirror_z(sums[0:16] + sums[16:32])
    for a in range(3):
        virial_out[3 * a:3 * a + 3, :] = sums[4 * a + 1:4 * a + 4]

    for g in range(8):
        answers[g].wait_recv()
    quarter = iota((8, 128), 1) >> 5
    tiles = []
    for u in range(2):
        tile = ret[4 * u]
        for v in range(1, 4):
            tile = jnp.where(quarter == v, ret[4 * u + v], tile)
        tiles.append(tile)
    back = jnp.concatenate(tiles, axis=1)
    parts = []
    for _ in range(3):
        parts.append(back.astype(BF16).astype(F32))
        back = back - parts[-1]
    spread_out = lax.dot_general(
        jnp.concatenate(parts, axis=0).astype(BF16), R[...], NN, preferred_element_type=F32)
    total = fo[:, 0:2048] + spread_out[0:8] + spread_out[8:16] + spread_out[16:24]
    field_out[...] = total[0:4]

    for g in range(8):
        halo[g].wait_send()
        guests[g].wait_send()
        answers[g].wait_send()


def hand_on(*refs):
    sem = refs[-1]
    copies = [pltpu.make_async_copy(refs[i], refs[3 + i], sem.at[i]) for i in range(3)]
    for copy in copies:
        copy.start()
    for copy in copies:
        copy.wait()


def shards(mult, ops, table, ev, ions, owner, slot):
    nx, ny = lax.axis_size("xs"), lax.axis_size("ys")
    dma = pltpu.SemaphoreType.DMA
    vmem = pltpu.VMEM
    outs = (
        jax.ShapeDtypeStruct((121, 128), BF16),
        jax.ShapeDtypeStruct((4, 2048), F32),
        jax.ShapeDtypeStruct((9, 128), F32),
    )
    found = pl.pallas_call(
        functools.partial(kernel, nx, ny),
        out_shape=outs,
        in_specs=[pl.BlockSpec(memory_space=pl.ANY)] * 7,
        out_specs=[pl.BlockSpec(memory_space=pltpu.VMEM)] * 3,
        scratch_shapes=[
            vmem((121, 128), BF16), vmem((8, 128), jnp.int32), vmem((4, 2048), BF16),
            vmem((1, 2048), jnp.int32), vmem((1, 2048), jnp.int32),
            vmem((121, 4, 2048), BF16), vmem((121, 316, 121), BF16), vmem((122, 320, 128), F32),
            vmem((512, 2304), F32), vmem((256, 2048), BF16), vmem((128, 2304), BF16),
            vmem((10, 10, 8, 128), F32), vmem((128, 49 * 128), BF16),
            vmem((128, 128), BF16), vmem((8, 128, 128), BF16), vmem((256, 512), BF16), vmem((256, 512), BF16),
            vmem((2, 8, 128), F32), vmem((8, 8, 128), F32), vmem((512, 128), BF16), vmem((8, 2304), F32),
            dma((6,)), dma((4,)), dma((8,)), dma((8,)), dma((8,)), dma((8,)), dma((8,)), dma((8,)),
        ],
        compiler_params=pltpu.CompilerParams(
            collective_id=0, has_side_effects=True, vmem_limit_bytes=58 * 2**20),
    )(
        mult,
        jnp.transpose(ops, (1, 0, 2)),
        table,
        jnp.transpose(ev, (1, 0, 2)),
        ions,
        jnp.reshape(owner, (1, owner.shape[0])),
        jnp.reshape(slot, (1, slot.shape[0])),
    )
    return pl.pallas_call(
        hand_on,
        out_shape=outs,
        in_specs=[pl.BlockSpec(memory_space=pl.ANY)] * 3,
        out_specs=[pl.BlockSpec(memory_space=pl.ANY)] * 3,
        scratch_shapes=[dma((3,))],
    )(*found)


def solution(mesh):
    both = ("xs", "ys")
    placed = (
        P(None, both),
        P(),
        P(None, both),
        P(None, None, both),
        P(None, both),
        P(both, None),
        P(both),
    )
    return jax.shard_map(
        shards,
        mesh=mesh,
        in_specs=placed,
        out_specs=(P(None, both), P(None, both), P(None, both)),
        check_vma=False,
    )
```

```python
import functools

import jax
import jax.numpy as jnp
from jax import lax
from jax.experimental import pallas as pl
from jax.experimental.pallas import tpu as pltpu
from jax.sharding import PartitionSpec as P

MESH = pl.DeviceIdType.MESH
NT = (((1,), (1,)), ((), ()))
NN = (((1,), (0,)), ((), ()))
F32 = jnp.float32
BF16 = jnp.bfloat16

AROUND = [(ex, ey) for ex in (-1, 0, 1) for ey in (-1, 0, 1) if (ex, ey) != (0, 0)]


def offset_columns():
    listed, row = [], 0
    for dx in range(-3, 4):
        for dy in range(-3, 4):
            near = abs(dx) <= 1 and abs(dy) <= 1
            listed.append((dx, dy, row, near))
            row += 4 if near else 7
    return listed


COLUMNS = sorted(offset_columns(), key=lambda c: 2 if c[3] else c[2] % 2)
GROUP = [2 if c[3] else c[2] % 2 for c in COLUMNS]
SPANS = [(GROUP.index(g), GROUP.index(g) + GROUP.count(g)) for g in range(3)]
SELF_ROW = [c[2] for c in COLUMNS if c[:2] == (0, 0)][0] + 1
CHUNKS = [(0, 32), (32, 32), (64, 32), (96, 25)]


def iota(shape, axis):
    return lax.broadcasted_iota(jnp.int32, shape, axis)


def one_hot(condition):
    return jnp.where(condition, 1.0, 0.0).astype(BF16)


def mirror_z(x):
    axis = x.ndim - 1
    lane = iota(x.shape, axis)
    for bit in (1, 2, 4):
        x = jnp.where((lane & bit) != 0, pltpu.roll(x, bit, axis), pltpu.roll(x, 128 - bit, axis))
    return x


def kernel(
    nx, ny,
    mult, ops, table, ev, ions, owner, slot,
    local_out, field_out, virial_out,
    mraw, trow, iraw, oraw, sraw, eb, tb, Ef, R, OH, ext, G,
    msend, mrecv, ec, gmsg, fg, ret, Lrep, fo,
    in_sem, op_sem, s1, r1, s2, r2, s3, r3,
):
    mx = lax.axis_index("xs")
    my = lax.axis_index("ys")

    def peer(g):
        ex, ey = AROUND[g]
        return (lax.rem(mx + ex + nx, nx), lax.rem(my + ey + ny, ny))

    first = SELF_ROW // 8 * 8
    loads = [
        pltpu.make_async_copy(mult, mraw, in_sem.at[0]),
        pltpu.make_async_copy(table.at[pl.ds(first, 8)], trow, in_sem.at[1]),
        pltpu.make_async_copy(owner, oraw, in_sem.at[2]),
        pltpu.make_async_copy(slot, sraw, in_sem.at[3]),
        pltpu.make_async_copy(ions, iraw, in_sem.at[4]),
        pltpu.make_async_copy(ev, eb, in_sem.at[5]),
    ]
    for copy in loads:
        copy.start()
    op_loads = [
        pltpu.make_async_copy(ops.at[pl.ds(q0, n)], tb.at[pl.ds(q0, n)], op_sem.at[c])
        for c, (q0, n) in enumerate(CHUNKS)
    ]
    barrier = pltpu.get_barrier_semaphore()
    for g in range(8):
        pl.semaphore_signal(barrier, inc=1, device_id=peer(g), device_id_type=MESH)

    loads[0].wait()
    loads[1].wait()
    for copy in op_loads:
        copy.start()
    named = trow[SELF_ROW - first:SELF_ROW - first + 1, :]
    lane = iota((1, 128), 1)
    named = jnp.where((lane & 7) < 6, pltpu.roll(named, 126, 1), pltpu.roll(named, 6, 1))
    filled = named >= 0
    pick = one_hot((iota((128, 128), 0) == (iota((128, 128), 1) ^ 7)) & jnp.broadcast_to(filled, (128, 128)))
    turned = lax.dot_general(pick, mraw[...], NT, preferred_element_type=F32)
    msend[...] = jnp.zeros_like(msend)
    msend[:, 0:121] = turned.astype(BF16)

    pl.semaphore_wait(barrier, 8)
    halo = []
    for g in range(8):
        ex = AROUND[g][0]
        rows = pl.ds(32 if ex < 0 else 0, 128 if ex == 0 else 96)
        halo.append(pltpu.make_async_remote_copy(
            src_ref=msend.at[rows], dst_ref=mrecv.at[g, rows], send_sem=s1.at[g], recv_sem=r1.at[g],
            device_id=peer(7 - g), device_id_type=MESH))
        halo[-1].start()

    loads[2].wait()
    loads[3].wait()
    own_id = oraw[...]
    shift = ny.bit_length() - 1
    step_x = (((own_id >> shift) - mx + 1 + nx) & (nx - 1)) - 1
    step_y = (((own_id & (ny - 1)) - my + 1 + ny) & (ny - 1)) - 1
    towards = 3 * (step_x + 1) + step_y + 1
    here = towards == 4
    group = jnp.where(here, -1, 7 - jnp.where(towards > 4, towards - 1, towards))
    member = jnp.where(iota((8, 2048), 0) == group, 1.0, 0.0)
    stacked = jnp.concatenate([member[:, 128 * b:128 * b + 128] for b in range(16)], axis=0)
    stacked_b = stacked.astype(BF16)
    row, col = iota((128, 128), 0), iota((128, 128), 1)
    before = one_hot(row < col)
    earlier = one_hot(((row & 7) == (col & 7)) & ((col >> 3) < (row >> 3)))
    ones = jnp.ones((128, 128), BF16)
    counts = lax.dot_general(earlier, stacked_b, NN, preferred_element_type=F32).astype(BF16)
    rank = lax.dot_general(stacked_b, before, NN, preferred_element_type=F32)
    rank = rank + lax.dot_general(counts, ones, NN, preferred_element_type=F32)
    place = stacked * (rank + (32 * (row & 7) + 1).astype(F32))
    place = jnp.sum(place.reshape(16, 8, 128), axis=1, keepdims=True) - 1.0
    row_f = iota((256, 128), 0).astype(F32)
    for b in range(16):
        R[:, 128 * b:128 * b + 128] = one_hot(row_f == place[b])
    own_slot = sraw[...]
    OH[:, 0:2048] = one_hot(iota((128, 2048), 0) == jnp.where(here, own_slot ^ 7, -1))

    loads[4].wait()
    loads[5].wait()

    def spread(i, _):
        both = jnp.concatenate([eb[2 * i].astype(F32), eb[2 * i + 1].astype(F32)], axis=0)
        Ef[pl.ds(pl.multiple_of(8 * i, 8), 8), 0:2048] = both
        return 0

    lax.fori_loop(0, 60, spread, 0, unroll=4)
    Ef[480:488, 0:2048] = jnp.concatenate([eb[120].astype(F32), iraw[...].astype(F32)], axis=0)
    Ef[488:496, 0:2048] = jnp.where(iota((8, 2048), 0) == 0, own_slot.astype(F32), 0.0)
    Ef[496:512, 0:2048] = jnp.zeros((16, 2048), F32)

    ec[...] = lax.dot_general(
        R[...], Ef[:, 0:2048].astype(BF16), NT, preferred_element_type=F32).astype(BF16)
    guests = []
    for g in range(8):
        rows = pl.ds(32 * g, 32)
        guests.append(pltpu.make_async_remote_copy(
            src_ref=ec.at[rows], dst_ref=gmsg.at[rows], send_sem=s2.at[g], recv_sem=r2.at[g],
            device_id=peer(7 - g), device_id_type=MESH))
        guests[-1].start()

    def place_block(block, ex, ey):
        block = block.astype(F32).reshape(4, 4, 8, 128)
        sx = {-1: (1, 4, 0), 0: (0, 4, 3), 1: (0, 3, 7)}[ex]
        sy = {-1: (1, 4, 0), 0: (0, 4, 3), 1: (0, 3, 7)}[ey]
        ext[sx[2]:sx[2] + sx[1] - sx[0], sy[2]:sy[2] + sy[1] - sy[0]] = block[sx[0]:sx[1], sy[0]:sy[1]]

    place_block(msend[...], 0, 0)
    for g in range(8):
        halo[g].wait_recv()
        place_block(mrecv[g], *AROUND[g])
    grid_x, grid_y = iota((4, 4, 8, 128), 0), iota((4, 4, 8, 128), 1)
    for j, (dx, dy, _, _) in enumerate(COLUMNS):
        block = ext[dx + 3:dx + 7, dy + 3:dy + 7]
        if abs(dx) == 3:
            block = jnp.where((grid_x & 1) == (0 if dx > 0 else 1), block, 0.0)
        if abs(dy) == 3:
            block = jnp.where((grid_y & 1) == (0 if dy > 0 else 1), block, 0.0)
        G[:, 128 * j:128 * j + 128] = block.reshape(128, 128).astype(BF16)

    def weights(q0, n, j):
        k0 = COLUMNS[j][2] // 2 * 2
        rows = tb[q0:q0 + n, k0:k0 + 8, :].reshape(8 * n, 121)
        return jnp.concatenate([rows, jnp.zeros((8 * n, 7), BF16)], axis=1)

    def translate(c, beside):
        q0, n = CHUNKS[c]
        q0, n = q0 - n % 2, n + n % 2
        totals, step = [], 0
        for low, high in SPANS:
            total = jnp.zeros((8 * n, 128), F32)
            for j in range(low, high, 2):
                w = weights(q0, n, j)
                width = 128
                if j + 1 < high:
                    w = jnp.concatenate([w, weights(q0, n, j + 1)], axis=1)
                    width = 256
                total = total + lax.dot_general(
                    w, G[:, 128 * j:128 * j + width], NT, preferred_element_type=F32)
                step += 1
                if step == 4:
                    beside()
            totals.append(total.reshape(n, 8, 128))
        return totals

    def settle(c, totals):
        q0, n = CHUNKS[c]
        rows = (n + 3) // 4 * 4
        if n % 2:
            totals = [jnp.concatenate([t[1:], jnp.zeros((rows - n, 8, 128), F32)], axis=0) for t in totals]
        cell = (rows, 8, 128)
        at = iota(cell, 1)
        even, odd, near = totals
        total = even + pltpu.roll(odd, 7, 1)
        total = total + jnp.where(at < 2, near, jnp.where((at == 5) | (at == 6), pltpu.roll(near, 3, 1), 0.0))
        dz = at - 3
        source_z = (iota(cell, 2) & 7) - dz
        inside = (source_z >= 0) & (source_z <= 7)
        odd_z = (iota(cell, 2) & 1) == 0
        valid = (jnp.abs(dz) < 3) | ((dz == -3) & odd_z) | ((dz == 3) & jnp.logical_not(odd_z))
        skewed = pltpu.roll(total, 0, 2, stride=1, stride_axis=1)
        turned = pltpu.roll(skewed, 125, 2)
        wrapped = jnp.where(dz > 0, pltpu.roll(skewed, 117, 2), pltpu.roll(skewed, 5, 2))
        picked = jnp.where(valid, jnp.where(inside, turned, wrapped), 0.0)
        sums = jnp.sum(picked, axis=1, keepdims=True)
        wide = jnp.broadcast_to(sums, cell).reshape(rows // 2, 2, 8, 128)
        wide = jnp.where(iota((rows // 2, 8, 128), 1) < 4, wide[:, 0], wide[:, 1]).reshape(4 * rows, 128)
        Lrep[4 * q0:4 * q0 + 4 * rows, :] = wide.astype(BF16)
        return sums.reshape(rows, 128)

    def put_local(c, sums):
        q0, n = CHUNKS[c]
        local_out[q0:q0 + n, :] = mirror_z(sums)[0:n].astype(BF16)

    assert all(c[2] % 2 == 0 for c in COLUMNS if c[3])
    op_loads[0].wait()
    done = translate(0, lambda: None)
    op_loads[1].wait()
    op_loads[2].wait()
    for c in (1, 2):
        before_it = done
        done = translate(c, lambda: put_local(c - 1, settle(c - 1, before_it)))

    for g in range(8):
        guests[g].wait_recv()
    received = gmsg[...].astype(F32)
    for c in range(4):
        Ef[128 * c:128 * c + 128, 2048:2304] = jnp.transpose(received[:, 128 * c:128 * c + 128])
    guest_slot = Ef[488:489, 2048:2304].astype(jnp.int32) ^ 7
    OH[:, 2048:2304] = one_hot(iota((128, 256), 0) == guest_slot)

    op_loads[3].wait()
    last = settle(3, translate(3, lambda: put_local(2, settle(2, done))))

    def evaluate(start):
        values = lax.dot_general(
            Lrep[0:496, :], OH[:, start:start + 256], NN, preferred_element_type=F32)
        values = values * Ef[0:496, start:start + 256]
        total = jnp.sum(values.reshape(62, 8, 256), axis=0)
        return total + pltpu.roll(total, 4, 0)

    far = evaluate(2048)
    fo[:, 2048:2304] = far
    fg[0] = far[:, 0:128]
    fg[1] = far[:, 128:256]
    answers = []
    for g in range(8):
        answers.append(pltpu.make_async_remote_copy(
            src_ref=fg.at[g // 4], dst_ref=ret.at[g], send_sem=s3.at[g], recv_sem=r3.at[g],
            device_id=peer(g), device_id_type=MESH))
        answers[-1].start()
    put_local(3, last)
    for b in range(8):
        fo[:, 256 * b:256 * b + 256] = evaluate(256 * b)

    field = fo[...]
    charge = Ef[484:485, :]
    low = iota((8, 2304), 0) < 4
    arm = jnp.where(low, charge * Ef[485:486, :], charge * Ef[486:487, :])
    terms = jnp.concatenate([arm * field, charge * Ef[487:488, :] * field], axis=0)
    high = terms.astype(BF16)
    rest = (terms - high.astype(F32)).astype(BF16)
    sums = lax.dot_general(jnp.concatenate([high, rest], axis=0), OH[...], NT, preferred_element_type=F32)
    sums = mirror_z(sums[0:16] + sums[16:32])
    for a in range(3):
        virial_out[3 * a:3 * a + 3, :] = sums[4 * a + 1:4 * a + 4]

    for g in range(8):
        answers[g].wait_recv()
    quarter = iota((8, 128), 1) >> 5
    tiles = []
    for u in range(2):
        tile = ret[4 * u]
        for v in range(1, 4):
            tile = jnp.where(quarter == v, ret[4 * u + v], tile)
        tiles.append(tile)
    back = jnp.concatenate(tiles, axis=1)
    parts = []
    for _ in range(3):
        parts.append(back.astype(BF16).astype(F32))
        back = back - parts[-1]
    spread_out = lax.dot_general(
        jnp.concatenate(parts, axis=0).astype(BF16), R[...], NN, preferred_element_type=F32)
    total = fo[:, 0:2048] + spread_out[0:8] + spread_out[8:16] + spread_out[16:24]
    field_out[...] = total[0:4]

    for g in range(8):
        halo[g].wait_send()
        guests[g].wait_send()
        answers[g].wait_send()


def hand_on(*refs):
    sem = refs[-1]
    copies = [pltpu.make_async_copy(refs[i], refs[3 + i], sem.at[i]) for i in range(3)]
    for copy in copies:
        copy.start()
    for copy in copies:
        copy.wait()


def shards(mult, ops, table, ev, ions, owner, slot):
    nx, ny = lax.axis_size("xs"), lax.axis_size("ys")
    dma = pltpu.SemaphoreType.DMA
    vmem = pltpu.VMEM
    outs = (
        jax.ShapeDtypeStruct((121, 128), BF16),
        jax.ShapeDtypeStruct((4, 2048), F32),
        jax.ShapeDtypeStruct((9, 128), F32),
    )
    found = pl.pallas_call(
        functools.partial(kernel, nx, ny),
        out_shape=(vmem((121, 128), BF16), vmem((4, 2048), F32), vmem((9, 128), F32)),
        in_specs=[pl.BlockSpec(memory_space=pl.ANY)] * 7,
        out_specs=[pl.BlockSpec(memory_space=pltpu.VMEM)] * 3,
        scratch_shapes=[
            vmem((121, 128), BF16), vmem((8, 128), jnp.int32), vmem((4, 2048), BF16),
            vmem((1, 2048), jnp.int32), vmem((1, 2048), jnp.int32),
            vmem((121, 4, 2048), BF16), vmem((121, 316, 121), BF16),
            vmem((512, 2304), F32), vmem((256, 2048), BF16), vmem((128, 2304), BF16),
            vmem((10, 10, 8, 128), F32), vmem((128, 49 * 128), BF16),
            vmem((128, 128), BF16), vmem((8, 128, 128), BF16), vmem((256, 512), BF16), vmem((256, 512), BF16),
            vmem((2, 8, 128), F32), vmem((8, 8, 128), F32), vmem((512, 128), BF16), vmem((8, 2304), F32),
            dma((6,)), dma((4,)), dma((8,)), dma((8,)), dma((8,)), dma((8,)), dma((8,)), dma((8,)),
        ],
        compiler_params=pltpu.CompilerParams(
            collective_id=0, has_side_effects=True, vmem_limit_bytes=58 * 2**20),
    )(
        mult,
        jnp.transpose(ops, (1, 0, 2)),
        table,
        jnp.transpose(ev, (1, 0, 2)),
        ions,
        jnp.reshape(owner, (1, owner.shape[0])),
        jnp.reshape(slot, (1, slot.shape[0])),
    )
    return pl.pallas_call(
        hand_on,
        out_shape=outs,
        in_specs=[pl.BlockSpec(memory_space=pltpu.VMEM)] * 3,
        out_specs=[pl.BlockSpec(memory_space=pl.ANY)] * 3,
        scratch_shapes=[dma((3,))],
    )(*[pltpu.with_memory_space_constraint(x, pltpu.VMEM) for x in found])


def solution(mesh):
    both = ("xs", "ys")
    placed = (
        P(None, both),
        P(),
        P(None, both),
        P(None, None, both),
        P(None, both),
        P(both, None),
        P(both),
    )
    return jax.shard_map(
        shards,
        mesh=mesh,
        in_specs=placed,
        out_specs=(P(None, both), P(None, both), P(None, both)),
        check_vma=False,
    )
```

```python
import functools

import jax
import jax.numpy as jnp
from jax import lax
from jax.experimental import pallas as pl
from jax.experimental.pallas import tpu as pltpu
from jax.sharding import PartitionSpec as P

MESH = pl.DeviceIdType.MESH
NT = (((1,), (1,)), ((), ()))
NN = (((1,), (0,)), ((), ()))
F32 = jnp.float32
BF16 = jnp.bfloat16

AROUND = [(ex, ey) for ex in (-1, 0, 1) for ey in (-1, 0, 1) if (ex, ey) != (0, 0)]
FAR_FIRST = (0, 2, 5, 7, 1, 6, 3, 4)


def offset_columns():
    listed, row = [], 0
    for dx in range(-3, 4):
        for dy in range(-3, 4):
            near = abs(dx) <= 1 and abs(dy) <= 1
            listed.append((dx, dy, row, near))
            row += 4 if near else 7
    return listed


COLUMNS = sorted(offset_columns(), key=lambda c: 2 if c[3] else c[2] % 2)
GROUP = [2 if c[3] else c[2] % 2 for c in COLUMNS]
SPANS = [(GROUP.index(g), GROUP.index(g) + GROUP.count(g)) for g in range(3)]
SELF_ROW = [c[2] for c in COLUMNS if c[:2] == (0, 0)][0] + 1
CHUNKS = [(0, 32), (32, 32), (64, 32), (96, 25)]


def iota(shape, axis):
    return lax.broadcasted_iota(jnp.int32, shape, axis)


def one_hot(condition):
    return jnp.where(condition, 1.0, 0.0).astype(BF16)


def mirror_z(x):
    axis = x.ndim - 1
    lane = iota(x.shape, axis)
    for bit in (1, 2, 4):
        x = jnp.where((lane & bit) != 0, pltpu.roll(x, bit, axis), pltpu.roll(x, 128 - bit, axis))
    return x


def kernel(
    nx, ny,
    mult, ops, table, ev, ions, owner, slot,
    local_out, field_out, virial_out,
    mraw, trow, iraw, oraw, sraw, eb, tb, Ef, R, OH, ext, G,
    msend, mrecv, ec, gmsg, fg, ret, Lrep, fo,
    in_sem, op_sem, s1, r1, s2, r2, s3, r3,
):
    mx = lax.axis_index("xs")
    my = lax.axis_index("ys")

    def peer(g):
        ex, ey = AROUND[g]
        return (lax.rem(mx + ex + nx, nx), lax.rem(my + ey + ny, ny))

    first = SELF_ROW // 8 * 8
    loads = [
        pltpu.make_async_copy(mult, mraw, in_sem.at[0]),
        pltpu.make_async_copy(table.at[pl.ds(first, 8)], trow, in_sem.at[1]),
        pltpu.make_async_copy(owner, oraw, in_sem.at[2]),
        pltpu.make_async_copy(slot, sraw, in_sem.at[3]),
        pltpu.make_async_copy(ions, iraw, in_sem.at[4]),
        pltpu.make_async_copy(ev, eb, in_sem.at[5]),
    ]
    for copy in loads[:2]:
        copy.start()
    barrier = pltpu.get_barrier_semaphore()
    for g in FAR_FIRST:
        pl.semaphore_signal(barrier, inc=1, device_id=peer(g), device_id_type=MESH)

    for copy in loads[2:]:
        copy.start()
    op_loads = [
        pltpu.make_async_copy(ops.at[pl.ds(q0, n)], tb.at[pl.ds(q0, n)], op_sem.at[c])
        for c, (q0, n) in enumerate(CHUNKS)
    ]
    loads[0].wait()
    loads[1].wait()
    for copy in op_loads:
        copy.start()
    named = trow[SELF_ROW - first:SELF_ROW - first + 1, :]
    lane = iota((1, 128), 1)
    named = jnp.where((lane & 7) < 6, pltpu.roll(named, 126, 1), pltpu.roll(named, 6, 1))
    filled = named >= 0
    pick = one_hot((iota((128, 128), 0) == (iota((128, 128), 1) ^ 7)) & jnp.broadcast_to(filled, (128, 128)))
    turned = lax.dot_general(pick, mraw[...], NT, preferred_element_type=F32)
    msend[...] = jnp.zeros_like(msend)
    msend[:, 0:121] = turned.astype(BF16)

    pl.semaphore_wait(barrier, 8)
    halo = [None] * 8
    for g in FAR_FIRST:
        ex = AROUND[g][0]
        rows = pl.ds(64 if ex < 0 else 0, 128 if ex == 0 else 64)
        halo[g] = pltpu.make_async_remote_copy(
            src_ref=msend.at[rows], dst_ref=mrecv.at[g, rows], send_sem=s1.at[g], recv_sem=r1.at[g],
            device_id=peer(7 - g), device_id_type=MESH)
        halo[g].start()

    loads[2].wait()
    loads[3].wait()
    own_id = oraw[...]
    shift = ny.bit_length() - 1
    step_x = (((own_id >> shift) - mx + 1 + nx) & (nx - 1)) - 1
    step_y = (((own_id & (ny - 1)) - my + 1 + ny) & (ny - 1)) - 1
    towards = 3 * (step_x + 1) + step_y + 1
    here = towards == 4
    group = jnp.where(here, -1, 7 - jnp.where(towards > 4, towards - 1, towards))
    member = jnp.where(iota((8, 2048), 0) == group, 1.0, 0.0)
    stacked = jnp.concatenate([member[:, 128 * b:128 * b + 128] for b in range(16)], axis=0)
    stacked_b = stacked.astype(BF16)
    row, col = iota((128, 128), 0), iota((128, 128), 1)
    before = one_hot(row < col)
    earlier = one_hot(((row & 7) == (col & 7)) & ((col >> 3) < (row >> 3)))
    ones = jnp.ones((128, 128), BF16)
    counts = lax.dot_general(earlier, stacked_b, NN, preferred_element_type=F32).astype(BF16)
    rank = lax.dot_general(stacked_b, before, NN, preferred_element_type=F32)
    rank = rank + lax.dot_general(counts, ones, NN, preferred_element_type=F32)
    place = stacked * (rank + (32 * (row & 7) + 1).astype(F32))
    place = jnp.sum(place.reshape(16, 8, 128), axis=1, keepdims=True) - 1.0
    row_f = iota((256, 128), 0).astype(F32)
    for b in range(16):
        R[:, 128 * b:128 * b + 128] = one_hot(row_f == place[b])
    own_slot = sraw[...]
    OH[:, 0:2048] = one_hot(iota((128, 2048), 0) == jnp.where(here, own_slot ^ 7, -1))

    loads[4].wait()
    loads[5].wait()

    def spread(i, _):
        both = jnp.concatenate([eb[2 * i].astype(F32), eb[2 * i + 1].astype(F32)], axis=0)
        Ef[pl.ds(pl.multiple_of(8 * i, 8), 8), 0:2048] = both
        return 0

    lax.fori_loop(0, 60, spread, 0, unroll=4)
    Ef[480:488, 0:2048] = jnp.concatenate([eb[120].astype(F32), iraw[...].astype(F32)], axis=0)
    Ef[488:496, 0:2048] = jnp.where(iota((8, 2048), 0) == 0, own_slot.astype(F32), 0.0)
    Ef[496:512, 0:2048] = jnp.zeros((16, 2048), F32)

    ec[...] = lax.dot_general(
        R[...], Ef[:, 0:2048].astype(BF16), NT, preferred_element_type=F32).astype(BF16)
    guests = [None] * 8
    for g in FAR_FIRST:
        rows = pl.ds(32 * g, 32)
        guests[g] = pltpu.make_async_remote_copy(
            src_ref=ec.at[rows], dst_ref=gmsg.at[rows], send_sem=s2.at[g], recv_sem=r2.at[g],
            device_id=peer(7 - g), device_id_type=MESH)
        guests[g].start()

    def place_block(block, ex, ey):
        block = block.astype(F32).reshape(4, 4, 8, 128)
        sx = {-1: (2, 4, 1), 0: (0, 4, 3), 1: (0, 2, 7)}[ex]
        sy = {-1: (2, 4, 1), 0: (0, 4, 3), 1: (0, 2, 7)}[ey]
        ext[sx[2]:sx[2] + sx[1] - sx[0], sy[2]:sy[2] + sy[1] - sy[0]] = block[sx[0]:sx[1], sy[0]:sy[1]]

    place_block(msend[...], 0, 0)
    for copy in op_loads:
        copy.wait()
    for g in (3, 4, 1, 6, 0, 2, 5, 7):
        halo[g].wait_recv()
        place_block(mrecv[g], *AROUND[g])
    grid_x, grid_y = iota((4, 4, 8, 128), 0), iota((4, 4, 8, 128), 1)
    for j, (dx, dy, _, _) in enumerate(COLUMNS):
        block = ext[dx + 3:dx + 7, dy + 3:dy + 7]
        if abs(dx) == 3:
            block = jnp.where((grid_x & 1) == (0 if dx > 0 else 1), block, 0.0)
        if abs(dy) == 3:
            block = jnp.where((grid_y & 1) == (0 if dy > 0 else 1), block, 0.0)
        G[:, 128 * j:128 * j + 128] = block.reshape(128, 128).astype(BF16)

    def weights(q0, n, j):
        k0 = COLUMNS[j][2] // 2 * 2
        rows = tb[q0:q0 + n, k0:k0 + 8, :].reshape(8 * n, 121)
        return jnp.concatenate([rows, jnp.zeros((8 * n, 7), BF16)], axis=1)

    def translate(c, beside):
        q0, n = CHUNKS[c]
        q0, n = q0 - n % 2, n + n % 2
        totals, step = [], 0
        for low, high in SPANS:
            total = jnp.zeros((8 * n, 128), F32)
            for j in range(low, high, 2):
                w = weights(q0, n, j)
                width = 128
                if j + 1 < high:
                    w = jnp.concatenate([w, weights(q0, n, j + 1)], axis=1)
                    width = 256
                total = total + lax.dot_general(
                    w, G[:, 128 * j:128 * j + width], NT, preferred_element_type=F32)
                step += 1
                if step == 4:
                    beside()
            totals.append(total.reshape(n, 8, 128))
        return totals

    def settle(c, totals):
        q0, n = CHUNKS[c]
        rows = (n + 3) // 4 * 4
        if n % 2:
            totals = [jnp.concatenate([t[1:], jnp.zeros((rows - n, 8, 128), F32)], axis=0) for t in totals]
        cell = (rows, 8, 128)
        at = iota(cell, 1)
        even, odd, near = totals
        total = even + pltpu.roll(odd, 7, 1)
        total = total + jnp.where(at < 2, near, jnp.where((at == 5) | (at == 6), pltpu.roll(near, 3, 1), 0.0))
        dz = at - 3
        source_z = (iota(cell, 2) & 7) - dz
        inside = (source_z >= 0) & (source_z <= 7)
        odd_z = (iota(cell, 2) & 1) == 0
        valid = (jnp.abs(dz) < 3) | ((dz == -3) & odd_z) | ((dz == 3) & jnp.logical_not(odd_z))
        skewed = pltpu.roll(total, 0, 2, stride=1, stride_axis=1)
        turned = pltpu.roll(skewed, 125, 2)
        wrapped = jnp.where(dz > 0, pltpu.roll(skewed, 117, 2), pltpu.roll(skewed, 5, 2))
        picked = jnp.where(valid, jnp.where(inside, turned, wrapped), 0.0)
        sums = jnp.sum(picked, axis=1, keepdims=True)
        wide = jnp.broadcast_to(sums, cell).reshape(rows // 2, 2, 8, 128)
        wide = jnp.where(iota((rows // 2, 8, 128), 1) < 4, wide[:, 0], wide[:, 1]).reshape(4 * rows, 128)
        Lrep[4 * q0:4 * q0 + 4 * rows, :] = wide.astype(BF16)
        return sums.reshape(rows, 128)

    def put_local(c, sums):
        q0, n = CHUNKS[c]
        local_out[q0:q0 + n, :] = mirror_z(sums)[0:n].astype(BF16)

    assert all(c[2] % 2 == 0 for c in COLUMNS if c[3])
    done = translate(0, lambda: None)
    for c in (1, 2):
        before_it = done
        done = translate(c, lambda: put_local(c - 1, settle(c - 1, before_it)))

    for g in range(8):
        guests[g].wait_recv()
    received = gmsg[...].astype(F32)
    for c in range(4):
        Ef[128 * c:128 * c + 128, 2048:2304] = jnp.transpose(received[:, 128 * c:128 * c + 128])
    guest_slot = Ef[488:489, 2048:2304].astype(jnp.int32) ^ 7
    OH[:, 2048:2304] = one_hot(iota((128, 256), 0) == guest_slot)

    last = settle(3, translate(3, lambda: put_local(2, settle(2, done))))

    def evaluate(start):
        values = lax.dot_general(
            Lrep[0:496, :], OH[:, start:start + 256], NN, preferred_element_type=F32)
        values = values * Ef[0:496, start:start + 256]
        total = jnp.sum(values.reshape(62, 8, 256), axis=0)
        return total + pltpu.roll(total, 4, 0)

    far = evaluate(2048)
    fo[:, 2048:2304] = far
    fg[0] = far[:, 0:128]
    fg[1] = far[:, 128:256]
    answers = [None] * 8
    for g in FAR_FIRST:
        answers[g] = pltpu.make_async_remote_copy(
            src_ref=fg.at[g // 4], dst_ref=ret.at[g], send_sem=s3.at[g], recv_sem=r3.at[g],
            device_id=peer(g), device_id_type=MESH)
        answers[g].start()
    put_local(3, last)
    for b in range(8):
        fo[:, 256 * b:256 * b + 256] = evaluate(256 * b)

    field = fo[...]
    charge = Ef[484:485, :]
    low = iota((8, 2304), 0) < 4
    arm = jnp.where(low, charge * Ef[485:486, :], charge * Ef[486:487, :])
    terms = jnp.concatenate([arm * field, charge * Ef[487:488, :] * field], axis=0)
    high = terms.astype(BF16)
    rest = (terms - high.astype(F32)).astype(BF16)
    sums = lax.dot_general(jnp.concatenate([high, rest], axis=0), OH[...], NT, preferred_element_type=F32)
    sums = mirror_z(sums[0:16] + sums[16:32])
    for a in range(3):
        virial_out[3 * a:3 * a + 3, :] = sums[4 * a + 1:4 * a + 4]

    for g in range(8):
        answers[g].wait_recv()
    quarter = iota((8, 128), 1) >> 5
    tiles = []
    for u in range(2):
        tile = ret[4 * u]
        for v in range(1, 4):
            tile = jnp.where(quarter == v, ret[4 * u + v], tile)
        tiles.append(tile)
    back = jnp.concatenate(tiles, axis=1)
    parts = []
    for _ in range(3):
        parts.append(back.astype(BF16).astype(F32))
        back = back - parts[-1]
    spread_out = lax.dot_general(
        jnp.concatenate(parts, axis=0).astype(BF16), R[...], NN, preferred_element_type=F32)
    total = fo[:, 0:2048] + spread_out[0:8] + spread_out[8:16] + spread_out[16:24]
    field_out[...] = total[0:4]

    for g in range(8):
        halo[g].wait_send()
        guests[g].wait_send()
        answers[g].wait_send()


def hand_on(*refs):
    sem = refs[-1]
    copies = [pltpu.make_async_copy(refs[i], refs[3 + i], sem.at[i]) for i in range(3)]
    for copy in copies:
        copy.start()
    for copy in copies:
        copy.wait()


def shards(mult, ops, table, ev, ions, owner, slot):
    nx, ny = lax.axis_size("xs"), lax.axis_size("ys")
    dma = pltpu.SemaphoreType.DMA
    vmem = pltpu.VMEM
    outs = (
        jax.ShapeDtypeStruct((121, 128), BF16),
        jax.ShapeDtypeStruct((4, 2048), F32),
        jax.ShapeDtypeStruct((9, 128), F32),
    )
    found = pl.pallas_call(
        functools.partial(kernel, nx, ny),
        out_shape=(vmem((121, 128), BF16), vmem((4, 2048), F32), vmem((9, 128), F32)),
        in_specs=[pl.BlockSpec(memory_space=pl.ANY)] * 7,
        out_specs=[pl.BlockSpec(memory_space=pltpu.VMEM)] * 3,
        scratch_shapes=[
            vmem((121, 128), BF16), vmem((8, 128), jnp.int32), vmem((4, 2048), BF16),
            vmem((1, 2048), jnp.int32), vmem((1, 2048), jnp.int32),
            vmem((121, 4, 2048), BF16), vmem((121, 316, 121), BF16),
            vmem((512, 2304), F32), vmem((256, 2048), BF16), vmem((128, 2304), BF16),
            vmem((10, 10, 8, 128), F32), vmem((128, 49 * 128), BF16),
            vmem((128, 128), BF16), vmem((8, 128, 128), BF16), vmem((256, 512), BF16), vmem((256, 512), BF16),
            vmem((2, 8, 128), F32), vmem((8, 8, 128), F32), vmem((512, 128), BF16), vmem((8, 2304), F32),
            dma((6,)), dma((4,)), dma((8,)), dma((8,)), dma((8,)), dma((8,)), dma((8,)), dma((8,)),
        ],
        compiler_params=pltpu.CompilerParams(
            collective_id=0, has_side_effects=True, vmem_limit_bytes=58 * 2**20),
    )(
        mult,
        jnp.transpose(ops, (1, 0, 2)),
        table,
        jnp.transpose(ev, (1, 0, 2)),
        ions,
        jnp.reshape(owner, (1, owner.shape[0])),
        jnp.reshape(slot, (1, slot.shape[0])),
    )
    return pl.pallas_call(
        hand_on,
        out_shape=outs,
        in_specs=[pl.BlockSpec(memory_space=pltpu.VMEM)] * 3,
        out_specs=[pl.BlockSpec(memory_space=pl.ANY)] * 3,
        scratch_shapes=[dma((3,))],
    )(*[pltpu.with_memory_space_constraint(x, pltpu.VMEM) for x in found])


def solution(mesh):
    both = ("xs", "ys")
    placed = (
        P(None, both),
        P(),
        P(None, both),
        P(None, None, both),
        P(None, both),
        P(both, None),
        P(both),
    )
    return jax.shard_map(
        shards,
        mesh=mesh,
        in_specs=placed,
        out_specs=(P(None, both), P(None, both), P(None, both)),
        check_vma=False,
    )
```

```python
import functools

import jax
import jax.numpy as jnp
from jax import lax
from jax.experimental import pallas as pl
from jax.experimental.pallas import tpu as pltpu
from jax.sharding import PartitionSpec as P

MESH = pl.DeviceIdType.MESH
NT = (((1,), (1,)), ((), ()))
NN = (((1,), (0,)), ((), ()))
F32 = jnp.float32
BF16 = jnp.bfloat16

AROUND = [(ex, ey) for ex in (-1, 0, 1) for ey in (-1, 0, 1) if (ex, ey) != (0, 0)]
FAR_FIRST = (0, 2, 5, 7, 1, 6, 3, 4)


def offset_columns():
    listed, row = [], 0
    for dx in range(-3, 4):
        for dy in range(-3, 4):
            near = abs(dx) <= 1 and abs(dy) <= 1
            listed.append((dx, dy, row, near))
            row += 4 if near else 7
    return listed


def sort_key(column):
    dx, dy, row, near = column
    return (0 if dx == 0 or dy == 0 else 1, 2 if near else row % 2)


COLUMNS = sorted(offset_columns(), key=sort_key)
GROUP = [sort_key(c) for c in COLUMNS]
SPANS = [[(GROUP.index((s, g)), GROUP.index((s, g)) + GROUP.count((s, g))) for g in range(3)] for s in range(2)]
STRAIGHT = SPANS[1][0][0]
SELF_ROW = [c[2] for c in COLUMNS if c[:2] == (0, 0)][0] + 1
CHUNKS = [(0, 32), (32, 32), (64, 32), (96, 25)]


def iota(shape, axis):
    return lax.broadcasted_iota(jnp.int32, shape, axis)


def one_hot(condition):
    return jnp.where(condition, 1.0, 0.0).astype(BF16)


def mirror_z(x):
    axis = x.ndim - 1
    lane = iota(x.shape, axis)
    for bit in (1, 2, 4):
        x = jnp.where((lane & bit) != 0, pltpu.roll(x, bit, axis), pltpu.roll(x, 128 - bit, axis))
    return x


def kernel(
    nx, ny,
    mult, ops, table, ev, ions, owner, slot,
    local_out, field_out, virial_out,
    mraw, trow, iraw, oraw, sraw, eb, tb, Ef, R, OH, ext, G,
    part, msend, mrecv, ec, gmsg, fg, ret, Lrep, fo,
    in_sem, op_sem, s1, r1, s2, r2, s3, r3,
):
    mx = lax.axis_index("xs")
    my = lax.axis_index("ys")

    def peer(g):
        ex, ey = AROUND[g]
        return (lax.rem(mx + ex + nx, nx), lax.rem(my + ey + ny, ny))

    first = SELF_ROW // 8 * 8
    loads = [
        pltpu.make_async_copy(mult, mraw, in_sem.at[0]),
        pltpu.make_async_copy(table.at[pl.ds(first, 8)], trow, in_sem.at[1]),
        pltpu.make_async_copy(owner, oraw, in_sem.at[2]),
        pltpu.make_async_copy(slot, sraw, in_sem.at[3]),
        pltpu.make_async_copy(ions, iraw, in_sem.at[4]),
        pltpu.make_async_copy(ev, eb, in_sem.at[5]),
    ]
    for copy in loads[:2]:
        copy.start()
    barrier = pltpu.get_barrier_semaphore()
    for g in FAR_FIRST:
        pl.semaphore_signal(barrier, inc=1, device_id=peer(g), device_id_type=MESH)

    for copy in loads[2:]:
        copy.start()
    op_loads = [
        pltpu.make_async_copy(ops.at[pl.ds(q0, n)], tb.at[pl.ds(q0, n)], op_sem.at[c])
        for c, (q0, n) in enumerate(CHUNKS)
    ]
    loads[0].wait()
    loads[1].wait()
    for copy in op_loads:
        copy.start()
    named = trow[SELF_ROW - first:SELF_ROW - first + 1, :]
    lane = iota((1, 128), 1)
    named = jnp.where((lane & 7) < 6, pltpu.roll(named, 126, 1), pltpu.roll(named, 6, 1))
    filled = named >= 0
    pick = one_hot((iota((128, 128), 0) == (iota((128, 128), 1) ^ 7)) & jnp.broadcast_to(filled, (128, 128)))
    turned = lax.dot_general(pick, mraw[...], NT, preferred_element_type=F32)
    msend[...] = jnp.zeros_like(msend)
    msend[:, 0:121] = turned.astype(BF16)

    pl.semaphore_wait(barrier, 8)
    halo = [None] * 8
    for g in FAR_FIRST:
        ex = AROUND[g][0]
        rows = pl.ds(64 if ex < 0 else 0, 128 if ex == 0 else 64)
        halo[g] = pltpu.make_async_remote_copy(
            src_ref=msend.at[rows], dst_ref=mrecv.at[g, rows], send_sem=s1.at[g], recv_sem=r1.at[g],
            device_id=peer(7 - g), device_id_type=MESH)
        halo[g].start()

    loads[2].wait()
    loads[3].wait()
    own_id = oraw[...]
    shift = ny.bit_length() - 1
    step_x = (((own_id >> shift) - mx + 1 + nx) & (nx - 1)) - 1
    step_y = (((own_id & (ny - 1)) - my + 1 + ny) & (ny - 1)) - 1
    towards = 3 * (step_x + 1) + step_y + 1
    here = towards == 4
    group = jnp.where(here, -1, 7 - jnp.where(towards > 4, towards - 1, towards))
    member = jnp.where(iota((8, 2048), 0) == group, 1.0, 0.0)
    stacked = jnp.concatenate([member[:, 128 * b:128 * b + 128] for b in range(16)], axis=0)
    stacked_b = stacked.astype(BF16)
    row, col = iota((128, 128), 0), iota((128, 128), 1)
    before = one_hot(row < col)
    earlier = one_hot(((row & 7) == (col & 7)) & ((col >> 3) < (row >> 3)))
    ones = jnp.ones((128, 128), BF16)
    counts = lax.dot_general(earlier, stacked_b, NN, preferred_element_type=F32).astype(BF16)
    rank = lax.dot_general(stacked_b, before, NN, preferred_element_type=F32)
    rank = rank + lax.dot_general(counts, ones, NN, preferred_element_type=F32)
    place = stacked * (rank + (32 * (row & 7) + 1).astype(F32))
    place = jnp.sum(place.reshape(16, 8, 128), axis=1, keepdims=True) - 1.0
    row_f = iota((256, 128), 0).astype(F32)
    for b in range(16):
        R[:, 128 * b:128 * b + 128] = one_hot(row_f == place[b])
    own_slot = sraw[...]
    OH[:, 0:2048] = one_hot(iota((128, 2048), 0) == jnp.where(here, own_slot ^ 7, -1))

    loads[4].wait()
    loads[5].wait()

    def spread(i, _):
        both = jnp.concatenate([eb[2 * i].astype(F32), eb[2 * i + 1].astype(F32)], axis=0)
        Ef[pl.ds(pl.multiple_of(8 * i, 8), 8), 0:2048] = both
        return 0

    lax.fori_loop(0, 60, spread, 0, unroll=4)
    Ef[480:488, 0:2048] = jnp.concatenate([eb[120].astype(F32), iraw[...].astype(F32)], axis=0)
    Ef[488:496, 0:2048] = jnp.where(iota((8, 2048), 0) == 0, own_slot.astype(F32), 0.0)
    Ef[496:512, 0:2048] = jnp.zeros((16, 2048), F32)

    ec[...] = lax.dot_general(
        R[...], Ef[:, 0:2048].astype(BF16), NT, preferred_element_type=F32).astype(BF16)
    guests = [None] * 8
    for g in FAR_FIRST:
        rows = pl.ds(32 * g, 32)
        guests[g] = pltpu.make_async_remote_copy(
            src_ref=ec.at[rows], dst_ref=gmsg.at[rows], send_sem=s2.at[g], recv_sem=r2.at[g],
            device_id=peer(7 - g), device_id_type=MESH)
        guests[g].start()

    def place_block(block, ex, ey):
        block = block.astype(F32).reshape(4, 4, 8, 128)
        sx = {-1: (2, 4, 1), 0: (0, 4, 3), 1: (0, 2, 7)}[ex]
        sy = {-1: (2, 4, 1), 0: (0, 4, 3), 1: (0, 2, 7)}[ey]
        ext[sx[2]:sx[2] + sx[1] - sx[0], sy[2]:sy[2] + sy[1] - sy[0]] = block[sx[0]:sx[1], sy[0]:sy[1]]

    place_block(msend[...], 0, 0)
    for copy in op_loads:
        copy.wait()
    for g in (3, 4, 1, 6):
        halo[g].wait_recv()
        place_block(mrecv[g], *AROUND[g])
    grid_x, grid_y = iota((4, 4, 8, 128), 0), iota((4, 4, 8, 128), 1)

    def gather(j):
        dx, dy, _, _ = COLUMNS[j]
        block = ext[dx + 3:dx + 7, dy + 3:dy + 7]
        if abs(dx) == 3:
            block = jnp.where((grid_x & 1) == (0 if dx > 0 else 1), block, 0.0)
        if abs(dy) == 3:
            block = jnp.where((grid_y & 1) == (0 if dy > 0 else 1), block, 0.0)
        G[:, 128 * j:128 * j + 128] = block.reshape(128, 128).astype(BF16)

    for j in range(STRAIGHT):
        gather(j)

    def weights(q0, n, j):
        k0 = COLUMNS[j][2] // 2 * 2
        rows = tb[q0:q0 + n, k0:k0 + 8, :].reshape(8 * n, 121)
        return jnp.concatenate([rows, jnp.zeros((8 * n, 7), BF16)], axis=1)

    def translate(stage, c, totals, beside):
        q0, n = CHUNKS[c]
        q0, n = q0 - n % 2, n + n % 2
        step = 0
        for group, (low, high) in enumerate(SPANS[stage]):
            total = totals[group]
            for j in range(low, high, 2):
                w = weights(q0, n, j)
                width = 128
                if j + 1 < high:
                    w = jnp.concatenate([w, weights(q0, n, j + 1)], axis=1)
                    width = 256
                total = total + lax.dot_general(
                    w, G[:, 128 * j:128 * j + width], NT, preferred_element_type=F32)
                step += 1
                if step == 4:
                    beside()
            totals[group] = total
        return totals

    def finish(c, beside):
        n = CHUNKS[c][1] + CHUNKS[c][1] % 2
        totals = translate(1, c, [part[c, group, 0:8 * n, :] for group in range(3)], beside)
        return [total.reshape(n, 8, 128) for total in totals]

    for c in range(4):
        n = CHUNKS[c][1] + CHUNKS[c][1] % 2
        for group, total in enumerate(translate(0, c, [jnp.zeros((8 * n, 128), F32)] * 3, lambda: None)):
            part[c, group, 0:8 * n, :] = total
    for g in (0, 2, 5, 7):
        halo[g].wait_recv()
        place_block(mrecv[g], *AROUND[g])
    for j in range(STRAIGHT, 49):
        gather(j)

    def settle(c, totals):
        q0, n = CHUNKS[c]
        rows = (n + 3) // 4 * 4
        if n % 2:
            totals = [jnp.concatenate([t[1:], jnp.zeros((rows - n, 8, 128), F32)], axis=0) for t in totals]
        cell = (rows, 8, 128)
        at = iota(cell, 1)
        even, odd, near = totals
        total = even + pltpu.roll(odd, 7, 1)
        total = total + jnp.where(at < 2, near, jnp.where((at == 5) | (at == 6), pltpu.roll(near, 3, 1), 0.0))
        dz = at - 3
        source_z = (iota(cell, 2) & 7) - dz
        inside = (source_z >= 0) & (source_z <= 7)
        odd_z = (iota(cell, 2) & 1) == 0
        valid = (jnp.abs(dz) < 3) | ((dz == -3) & odd_z) | ((dz == 3) & jnp.logical_not(odd_z))
        skewed = pltpu.roll(total, 0, 2, stride=1, stride_axis=1)
        turned = pltpu.roll(skewed, 125, 2)
        wrapped = jnp.where(dz > 0, pltpu.roll(skewed, 117, 2), pltpu.roll(skewed, 5, 2))
        picked = jnp.where(valid, jnp.where(inside, turned, wrapped), 0.0)
        sums = jnp.sum(picked, axis=1, keepdims=True)
        wide = jnp.broadcast_to(sums, cell).reshape(rows // 2, 2, 8, 128)
        wide = jnp.where(iota((rows // 2, 8, 128), 1) < 4, wide[:, 0], wide[:, 1]).reshape(4 * rows, 128)
        Lrep[4 * q0:4 * q0 + 4 * rows, :] = wide.astype(BF16)
        return sums.reshape(rows, 128)

    def put_local(c, sums):
        q0, n = CHUNKS[c]
        local_out[q0:q0 + n, :] = mirror_z(sums)[0:n].astype(BF16)

    assert all(c[2] % 2 == 0 for c in COLUMNS if c[3])
    done = finish(0, lambda: None)
    for c in (1, 2):
        before_it = done
        done = finish(c, lambda: put_local(c - 1, settle(c - 1, before_it)))

    for g in range(8):
        guests[g].wait_recv()
    received = gmsg[...].astype(F32)
    for c in range(4):
        Ef[128 * c:128 * c + 128, 2048:2304] = jnp.transpose(received[:, 128 * c:128 * c + 128])
    guest_slot = Ef[488:489, 2048:2304].astype(jnp.int32) ^ 7
    OH[:, 2048:2304] = one_hot(iota((128, 256), 0) == guest_slot)

    last = settle(3, finish(3, lambda: put_local(2, settle(2, done))))

    def evaluate(start):
        values = lax.dot_general(
            Lrep[0:496, :], OH[:, start:start + 256], NN, preferred_element_type=F32)
        values = values * Ef[0:496, start:start + 256]
        total = jnp.sum(values.reshape(62, 8, 256), axis=0)
        return total + pltpu.roll(total, 4, 0)

    far = evaluate(2048)
    fo[:, 2048:2304] = far
    fg[0] = far[:, 0:128]
    fg[1] = far[:, 128:256]
    answers = [None] * 8
    for g in FAR_FIRST:
        answers[g] = pltpu.make_async_remote_copy(
            src_ref=fg.at[g // 4], dst_ref=ret.at[g], send_sem=s3.at[g], recv_sem=r3.at[g],
            device_id=peer(g), device_id_type=MESH)
        answers[g].start()
    put_local(3, last)
    for b in range(8):
        fo[:, 256 * b:256 * b + 256] = evaluate(256 * b)

    field = fo[...]
    charge = Ef[484:485, :]
    low = iota((8, 2304), 0) < 4
    arm = jnp.where(low, charge * Ef[485:486, :], charge * Ef[486:487, :])
    terms = jnp.concatenate([arm * field, charge * Ef[487:488, :] * field], axis=0)
    high = terms.astype(BF16)
    rest = (terms - high.astype(F32)).astype(BF16)
    sums = lax.dot_general(jnp.concatenate([high, rest], axis=0), OH[...], NT, preferred_element_type=F32)
    sums = mirror_z(sums[0:16] + sums[16:32])
    for a in range(3):
        virial_out[3 * a:3 * a + 3, :] = sums[4 * a + 1:4 * a + 4]

    for g in range(8):
        answers[g].wait_recv()
    quarter = iota((8, 128), 1) >> 5
    tiles = []
    for u in range(2):
        tile = ret[4 * u]
        for v in range(1, 4):
            tile = jnp.where(quarter == v, ret[4 * u + v], tile)
        tiles.append(tile)
    back = jnp.concatenate(tiles, axis=1)
    parts = []
    for _ in range(3):
        parts.append(back.astype(BF16).astype(F32))
        back = back - parts[-1]
    spread_out = lax.dot_general(
        jnp.concatenate(parts, axis=0).astype(BF16), R[...], NN, preferred_element_type=F32)
    total = fo[:, 0:2048] + spread_out[0:8] + spread_out[8:16] + spread_out[16:24]
    field_out[...] = total[0:4]

    for g in range(8):
        halo[g].wait_send()
        guests[g].wait_send()
        answers[g].wait_send()


def hand_on(*refs):
    sem = refs[-1]
    copies = [pltpu.make_async_copy(refs[i], refs[3 + i], sem.at[i]) for i in range(3)]
    for copy in copies:
        copy.start()
    for copy in copies:
        copy.wait()


def shards(mult, ops, table, ev, ions, owner, slot):
    nx, ny = lax.axis_size("xs"), lax.axis_size("ys")
    dma = pltpu.SemaphoreType.DMA
    vmem = pltpu.VMEM
    outs = (
        jax.ShapeDtypeStruct((121, 128), BF16),
        jax.ShapeDtypeStruct((4, 2048), F32),
        jax.ShapeDtypeStruct((9, 128), F32),
    )
    found = pl.pallas_call(
        functools.partial(kernel, nx, ny),
        out_shape=(vmem((121, 128), BF16), vmem((4, 2048), F32), vmem((9, 128), F32)),
        in_specs=[pl.BlockSpec(memory_space=pl.ANY)] * 7,
        out_specs=[pl.BlockSpec(memory_space=pltpu.VMEM)] * 3,
        scratch_shapes=[
            vmem((121, 128), BF16), vmem((8, 128), jnp.int32), vmem((4, 2048), BF16),
            vmem((1, 2048), jnp.int32), vmem((1, 2048), jnp.int32),
            vmem((121, 4, 2048), BF16), vmem((121, 316, 121), BF16),
            vmem((512, 2304), F32), vmem((256, 2048), BF16), vmem((128, 2304), BF16),
            vmem((10, 10, 8, 128), F32), vmem((128, 49 * 128), BF16), vmem((4, 3, 256, 128), F32),
            vmem((128, 128), BF16), vmem((8, 128, 128), BF16), vmem((256, 512), BF16), vmem((256, 512), BF16),
            vmem((2, 8, 128), F32), vmem((8, 8, 128), F32), vmem((512, 128), BF16), vmem((8, 2304), F32),
            dma((6,)), dma((4,)), dma((8,)), dma((8,)), dma((8,)), dma((8,)), dma((8,)), dma((8,)),
        ],
        compiler_params=pltpu.CompilerParams(
            collective_id=0, has_side_effects=True, vmem_limit_bytes=58 * 2**20),
    )(
        mult,
        jnp.transpose(ops, (1, 0, 2)),
        table,
        jnp.transpose(ev, (1, 0, 2)),
        ions,
        jnp.reshape(owner, (1, owner.shape[0])),
        jnp.reshape(slot, (1, slot.shape[0])),
    )
    return pl.pallas_call(
        hand_on,
        out_shape=outs,
        in_specs=[pl.BlockSpec(memory_space=pltpu.VMEM)] * 3,
        out_specs=[pl.BlockSpec(memory_space=pl.ANY)] * 3,
        scratch_shapes=[dma((3,))],
    )(*[pltpu.with_memory_space_constraint(x, pltpu.VMEM) for x in found])


def solution(mesh):
    both = ("xs", "ys")
    placed = (
        P(None, both),
        P(),
        P(None, both),
        P(None, None, both),
        P(None, both),
        P(both, None),
        P(both),
    )
    return jax.shard_map(
        shards,
        mesh=mesh,
        in_specs=placed,
        out_specs=(P(None, both), P(None, both), P(None, both)),
        check_vma=False,
    )
```
